32 devices in a mesh: chan: 8 (over z, x), tm: 4 (over y, core).
Axes of the slice: x: 2, y: 2, z: 4, core: 2. Of those that a mesh axis runs over, the one named last changes fastest.
Arguments:
- waveform: bfloat16 [1024, 49152], P('chan', 'tm'), may hold values from -6 to 6
- coords: int32 [2, 1024], replicated, may hold values from 0 to 9999
- directions: int32 [2, 2048], replicated, may hold values from -32 to 32
- bins: int32 [96], replicated, may hold values from 1 to 511
Outputs:
- beams: float32 [96, 2, 96, 2048], P('chan', None, 'tm')
The draws below stay inside these ranges and needn't reach their ends.
All inputs are finite; a program needn't handle non-finite values.
Results may differ from the reference program's by a relative error of at most 0.0045.
Values may be sent and summed in bfloat16 or wider, within the bound.
A program may use at most 128 MiB of HBM per device.

```python
import math
import jax
import jax.numpy as jnp
from jax import lax

FL = 1024
HOP = 512
NB = 96
BEAMS = 2048
CHANNELS = 1024
FRAMES = 96
SAMPLES = 49152


def plant(entries, stream_key, smallest, top_value):
    dims = entries.shape
    place = [jax.random.randint(jax.random.fold_in(stream_key, axis), (), 0, dims[axis]) for axis in range(len(dims))]
    entries = entries.at[tuple(place)].set(smallest)
    longest = dims.index(max(dims))
    place[longest] = (place[longest] + 1) % dims[longest]
    return entries.at[tuple(place)].set(top_value)


def block_scale(rng, extent, pieces, low, high):
    factor_of = 1.0
    for axis_at, shards_of in pieces:
        steps = jax.random.uniform(jax.random.fold_in(jax.random.fold_in(rng, 6), axis_at), (shards_of,), jnp.float32, low / len(pieces), high / len(pieces))
        factor_of = factor_of * jnp.repeat(jnp.exp(steps), extent[axis_at] // shards_of).reshape((-1,) + (1,) * (len(extent) - 1 - axis_at))
    return factor_of


def noise(own_key, extent, scale, reach, cuts=(), kind=jnp.bfloat16):
    factor_of = block_scale(own_key, extent, cuts, -0.22, 0.18) if cuts else 1.0
    drawn = jax.random.normal(own_key, extent, jnp.float32) * scale * factor_of
    return jnp.minimum(jnp.maximum(drawn, -reach), reach).astype(kind)


def setup_inputs(seed: int = 0) -> dict:
    keys = jax.random.split(jax.random.key(seed), 5)
    return {
        "waveform": noise(keys[0], (CHANNELS, SAMPLES), 1.0, 6.0, ((0, 8), (1, 4))),
        "coords": plant(jax.random.randint(keys[1], (2, CHANNELS), 0, 10000), jax.random.fold_in(keys[1], 1), 0, 9999).astype(jnp.int32),
        "directions": plant(jax.random.randint(keys[2], (2, BEAMS), -32, 33), jax.random.fold_in(keys[2], 1), -32, 32).astype(jnp.int32),
        "bins": plant(jax.random.randint(keys[3], (NB,), 1, FL // 2), jax.random.fold_in(keys[3], 1), 1, (FL // 2) - 1).astype(jnp.int32),
    }


phase_steps = 1048576

def dft_table(bins):
    sample_index = jnp.arange(FL, dtype=jnp.int32)
    product = jnp.mod(sample_index[:, None] * bins[None, :], FL)
    angle = product.astype(jnp.float32) * jnp.float32(2.0 * math.pi / FL)
    window = 0.5 - 0.5 * jnp.cos(sample_index.astype(jnp.float32) * jnp.float32(2.0 * math.pi / FL))
    norm_factor = jnp.float32(1.0 / math.sqrt(FL))
    real_cols = window[:, None] * jnp.cos(angle) * norm_factor
    imag_cols = -window[:, None] * jnp.sin(angle) * norm_factor
    return jnp.concatenate([real_cols, imag_cols], axis=1).astype(jnp.bfloat16)

def bin_beams(bin_value, real_part, imag_part, offsets):
    stacked_left = jnp.concatenate([jnp.concatenate([real_part, -imag_part], axis=1), jnp.concatenate([imag_part, real_part], axis=1)], axis=0)
    turns = jnp.mod(bin_value * jnp.mod(offsets, phase_steps), phase_steps)
    angle = turns.astype(jnp.float32) * jnp.float32(2.0 * math.pi / phase_steps)
    steering = jnp.concatenate([jnp.cos(angle), jnp.sin(angle)], axis=0).astype(jnp.bfloat16)
    return jnp.dot(stacked_left, steering, preferred_element_type=jnp.float32)

def reference(waveform, coords, directions, bins):
    channel_count = waveform.shape[0]
    transform = dft_table(bins)
    padded = jnp.concatenate([waveform, jnp.zeros((channel_count, HOP), jnp.bfloat16)], axis=1)
    halves = padded.reshape(channel_count, FRAMES + 1, HOP)
    front_half = halves[:, :-1].reshape(-1, HOP)
    back_half = halves[:, 1:].reshape(-1, HOP)
    spectra = jnp.dot(front_half, transform[:HOP], preferred_element_type=jnp.float32) + jnp.dot(back_half, transform[HOP:], preferred_element_type=jnp.float32)
    spectra = spectra.astype(jnp.bfloat16).reshape(channel_count, FRAMES, 2 * NB)
    by_bin = jnp.transpose(spectra, (2, 1, 0))
    offsets = coords[0][:, None] * directions[0][None, :] + coords[1][:, None] * directions[1][None, :]

    def single(member):
        bin_value, real_part, imag_part = member
        return bin_beams(bin_value, real_part, imag_part, offsets)
    summed = lax.map(single, (bins, by_bin[:NB], by_bin[NB:]))
    summed = summed * jnp.float32(1.0 / math.sqrt(channel_count))
    return summed.reshape(NB, 2, FRAMES, BEAMS)
```

```python
import functools
import math

import jax
import jax.numpy as jnp
import numpy as np
from jax import lax
from jax.experimental import pallas as pl
from jax.experimental.pallas import tpu as pltpu
from jax.sharding import PartitionSpec as P

FL = 1024
PHASE_STEPS = 1048576
LANES = 128
BEAM_TILE = 512


def half_angle_fit():
    r = 0.5 * np.cos(np.pi * (np.arange(2000) + 0.5) / 4000)
    w = r * r
    sine = np.polynomial.polynomial.polyfit(w, np.sqrt(2) * np.sin(np.pi * r) / r, 2)
    cosine = np.polynomial.polynomial.polyfit(w, np.sqrt(2) * np.cos(np.pi * r), 3)
    return [float(c) for c in sine], [float(c) for c in cosine]


def dft_table(bins, frame_length):
    sample_index = jnp.arange(frame_length, dtype=jnp.int32)
    product = jnp.mod(bins[:, None] * sample_index[None, :], frame_length)
    angle = product.astype(jnp.float32) * jnp.float32(2.0 * math.pi / frame_length)
    window = 0.5 - 0.5 * jnp.cos(
        sample_index.astype(jnp.float32) * jnp.float32(2.0 * math.pi / frame_length)
    )
    scaled = window[None, :]
    norm_factor = jnp.float32(1.0 / math.sqrt(frame_length))
    real_rows = scaled * jnp.cos(angle) * norm_factor
    imag_rows = -scaled * jnp.sin(angle) * norm_factor
    return jnp.concatenate([real_rows, imag_rows], axis=0).astype(jnp.bfloat16)


def spectra_kernel(table_ref, wave_ref, next_ref, out_ref, rows_ref):
    hop = FL // 2
    frames = wave_ref.shape[1] // hop
    bin_count = table_ref.shape[0] // 2
    for t in range(frames):
        if t < frames - 1:
            frame = wave_ref[:, t * hop : t * hop + FL]
        else:
            frame = jnp.concatenate([wave_ref[:, t * hop :], next_ref[...]], axis=1)
        part = lax.dot_general(
            table_ref[...], frame, (((1,), (1,)), ((), ())), preferred_element_type=jnp.float32
        )
        rows_ref[:, t, :] = part[:bin_count]
        rows_ref[:, frames + t, :] = part[bin_count:]
    out_ref[...] = rows_ref[...].astype(jnp.bfloat16)


def spectra_rows(table, waveform, following):
    channels, samples = waveform.shape
    frames = samples // (FL // 2)
    bin_count = table.shape[0] // 2
    return pl.pallas_call(
        spectra_kernel,
        out_shape=jax.ShapeDtypeStruct((bin_count, 2 * frames, channels), jnp.bfloat16),
        scratch_shapes=[pltpu.VMEM((bin_count, 2 * frames, channels), jnp.float32)],
        compiler_params=pltpu.CompilerParams(vmem_limit_bytes=32 * 2**20),
    )(table, waveform, following)


def beam_kernel(bins_ref, coords_ref, directions_ref, x_ref, out_ref, offsets_ref, cos_ref, sin_ref, *, scale):
    sine, cosine = half_angle_fit()
    sources, _, rows, width = x_ref.shape
    channels = sources * width
    step = 16

    @pl.when(pl.program_id(1) == 0)
    def _():
        @pl.loop(0, channels, step=step)
        def _(at):
            piece = pl.ds(at, step)
            offsets_ref[piece, :] = (
                coords_ref[piece, 0:1] * directions_ref[0:1, :] + coords_ref[piece, 1:2] * directions_ref[1:2, :]
            )

    turn = bins_ref[pl.program_id(1)] * (2**32 // PHASE_STEPS)
    frames = rows // 2
    by_cos = jnp.zeros((rows, out_ref.shape[2]), jnp.float32)
    by_sin = jnp.zeros((rows, out_ref.shape[2]), jnp.float32)
    group = 2
    for first in range(0, sources, group):
        for at in range(first * width, (first + group) * width, step):
            x = (offsets_ref[at : at + step, :] * turn).astype(jnp.float32) * 2.0**-32
            w = x * x
            s = ((sine[2] * w + sine[1]) * w + sine[0]) * x
            c = ((cosine[3] * w + cosine[2]) * w + cosine[1]) * w + cosine[0]
            cos_ref[at : at + step, :] = (1.0 - s * s).astype(jnp.bfloat16)
            sin_ref[at : at + step, :] = (s * c).astype(jnp.bfloat16)
        left = jnp.concatenate([x_ref[first + k, 0] for k in range(group)], axis=1)
        rows_of = slice(first * width, (first + group) * width)
        by_cos += jnp.dot(left, cos_ref[rows_of, :], preferred_element_type=jnp.float32)
        by_sin += jnp.dot(left, sin_ref[rows_of, :], preferred_element_type=jnp.float32)
    out_ref[0, :frames, :] = (by_cos[:frames] - by_sin[frames:]) * scale
    out_ref[0, frames:, :] = (by_cos[frames:] + by_sin[:frames]) * scale


def form_beams(own_bins, coords, directions, received):
    sources, bins_dev, rows, width = received.shape
    channels = sources * width
    beams = directions.shape[1]
    tile = min(BEAM_TILE, beams)
    scale = 1.0 / math.sqrt(channels)
    return pl.pallas_call(
        functools.partial(beam_kernel, scale=scale),
        out_shape=jax.ShapeDtypeStruct((bins_dev, rows, beams), jnp.float32),
        grid_spec=pltpu.PrefetchScalarGridSpec(
            num_scalar_prefetch=1,
            grid=(beams // tile, bins_dev),
            in_specs=[
                pl.BlockSpec((channels, 2), lambda j, f, s: (0, 0)),
                pl.BlockSpec((2, tile), lambda j, f, s: (0, j)),
                pl.BlockSpec((sources, 1, rows, width), lambda j, f, s: (0, f, 0, 0)),
            ],
            out_specs=pl.BlockSpec((1, rows, tile), lambda j, f, s: (f, 0, j)),
            scratch_shapes=[
                pltpu.VMEM((channels, tile), jnp.int32),
                pltpu.VMEM((channels, tile), jnp.bfloat16),
                pltpu.VMEM((channels, tile), jnp.bfloat16),
            ],
        ),
        compiler_params=pltpu.CompilerParams(vmem_limit_bytes=48 * 2**20),
    )(own_bins, coords.T, directions, received)


def on_device(waveform, coords, directions, bins):
    channels_dev = waveform.shape[0]
    hop_length = FL // 2
    frames_dev = waveform.shape[1] // hop_length
    chan_count = lax.axis_size("chan")
    tm_count = lax.axis_size("tm")
    bins_dev = bins.shape[0] // chan_count
    following = lax.ppermute(
        waveform[:, :hop_length], "tm", [(i, i - 1) for i in range(1, tm_count)]
    )
    table = dft_table(bins, FL)
    rows = spectra_rows(table, waveform, following)
    rows = rows.reshape(chan_count, bins_dev, 2 * frames_dev, channels_dev)
    received = lax.all_to_all(rows, "chan", 0, 0)
    own_bins = lax.dynamic_slice_in_dim(bins, lax.axis_index("chan") * bins_dev, bins_dev, 0)
    beams = form_beams(own_bins, coords, directions, received)
    return beams.reshape(bins_dev, 2, frames_dev, directions.shape[1])


def solution(mesh):
    return jax.shard_map(
        on_device,
        mesh=mesh,
        in_specs=(P("chan", "tm"), P(), P(), P()),
        out_specs=P("chan", None, "tm", None),
        check_vma=False,
    )
```

```python
import functools
import math

import jax
import jax.numpy as jnp
import numpy as np
from jax import lax
from jax.experimental import pallas as pl
from jax.experimental.pallas import tpu as pltpu
from jax.sharding import PartitionSpec as P

FL = 1024
PHASE_STEPS = 1048576
LANES = 128
BEAM_TILE = 512


def half_angle_fit():
    r = 0.5 * np.cos(np.pi * (np.arange(2000) + 0.5) / 4000)
    w = r * r
    sine = np.polynomial.polynomial.polyfit(w, np.sqrt(2) * np.sin(np.pi * r) / r, 2)
    cosine = np.polynomial.polynomial.polyfit(w, np.sqrt(2) * np.cos(np.pi * r), 3)
    return [float(c) for c in sine], [float(c) for c in cosine]


def dft_table(bins, frame_length):
    sample_index = jnp.arange(frame_length, dtype=jnp.int32)
    product = jnp.mod(bins[:, None] * sample_index[None, :], frame_length)
    angle = product.astype(jnp.float32) * jnp.float32(2.0 * math.pi / frame_length)
    window = 0.5 - 0.5 * jnp.cos(
        sample_index.astype(jnp.float32) * jnp.float32(2.0 * math.pi / frame_length)
    )
    scaled = window[None, :]
    norm_factor = jnp.float32(1.0 / math.sqrt(frame_length))
    real_rows = scaled * jnp.cos(angle) * norm_factor
    imag_rows = -scaled * jnp.sin(angle) * norm_factor
    return jnp.concatenate([real_rows, imag_rows], axis=0).astype(jnp.bfloat16)


def spectra_kernel(table_ref, wave_ref, next_ref, out_ref, rows_ref):
    hop = FL // 2
    frames = wave_ref.shape[1] // hop
    bin_count = table_ref.shape[0] // 2
    for t in range(frames):
        if t < frames - 1:
            frame = wave_ref[:, t * hop : t * hop + FL]
        else:
            frame = jnp.concatenate([wave_ref[:, t * hop :], next_ref[...]], axis=1)
        part = lax.dot_general(
            table_ref[...], frame, (((1,), (1,)), ((), ())), preferred_element_type=jnp.float32
        )
        rows_ref[:, t, :] = part[:bin_count]
        rows_ref[:, frames + t, :] = part[bin_count:]
    out_ref[...] = rows_ref[...].astype(jnp.bfloat16)


def spectra_rows(table, waveform, following):
    channels, samples = waveform.shape
    frames = samples // (FL // 2)
    bin_count = table.shape[0] // 2
    return pl.pallas_call(
        spectra_kernel,
        out_shape=jax.ShapeDtypeStruct((bin_count, 2 * frames, channels), jnp.bfloat16),
        scratch_shapes=[pltpu.VMEM((bin_count, 2 * frames, channels), jnp.float32)],
        compiler_params=pltpu.CompilerParams(vmem_limit_bytes=32 * 2**20),
    )(table, waveform, following)


def beam_kernel(bins_ref, coords_ref, directions_ref, x_ref, out_ref, offsets_ref, cos_ref, sin_ref, *, scale):
    sine, cosine = half_angle_fit()
    sources, _, rows, width = x_ref.shape
    channels = sources * width
    step = 16

    @pl.when(pl.program_id(1) == 0)
    def _():
        @pl.loop(0, channels, step=step)
        def _(at):
            piece = pl.ds(at, step)
            offsets_ref[piece, :] = (
                coords_ref[piece, 0:1] * directions_ref[0:1, :] + coords_ref[piece, 1:2] * directions_ref[1:2, :]
            )

    turn = bins_ref[pl.program_id(1)] * (2**32 // PHASE_STEPS)
    frames = rows // 2
    by_cos = jnp.zeros((rows, out_ref.shape[2]), jnp.float32)
    by_sin = jnp.zeros((rows, out_ref.shape[2]), jnp.float32)
    group = 2
    for first in range(0, sources, group):
        for at in range(first * width, (first + group) * width, step):
            x = (offsets_ref[at : at + step, :] * turn).astype(jnp.float32) * 2.0**-32
            w = x * x
            s = ((sine[2] * w + sine[1]) * w + sine[0]) * x
            c = ((cosine[3] * w + cosine[2]) * w + cosine[1]) * w + cosine[0]
            cos_ref[at : at + step, :] = (1.0 - s * s).astype(jnp.bfloat16)
            sin_ref[at : at + step, :] = (s * c).astype(jnp.bfloat16)
        left = jnp.concatenate([x_ref[first + k, 0] for k in range(group)], axis=1)
        rows_of = slice(first * width, (first + group) * width)
        by_cos += jnp.dot(left, cos_ref[rows_of, :], preferred_element_type=jnp.float32)
        by_sin += jnp.dot(left, sin_ref[rows_of, :], preferred_element_type=jnp.float32)
    out_ref[0, :frames, :] = (by_cos[:frames] - by_sin[frames:]) * scale
    out_ref[0, frames:, :] = (by_cos[frames:] + by_sin[:frames]) * scale


def form_beams(own_bins, coords, directions, received):
    sources, bins_dev, rows, width = received.shape
    channels = sources * width
    beams = directions.shape[1]
    tile = min(BEAM_TILE, beams)
    scale = 1.0 / math.sqrt(channels)
    return pl.pallas_call(
        functools.partial(beam_kernel, scale=scale),
        out_shape=jax.ShapeDtypeStruct((bins_dev, rows, beams), jnp.float32),
        grid_spec=pltpu.PrefetchScalarGridSpec(
            num_scalar_prefetch=1,
            grid=(beams // tile, bins_dev),
            in_specs=[
                pl.BlockSpec((channels, 2), lambda j, f, s: (0, 0)),
                pl.BlockSpec((2, tile), lambda j, f, s: (0, j)),
                pl.BlockSpec((sources, 1, rows, width), lambda j, f, s: (0, f, 0, 0)),
            ],
            out_specs=pl.BlockSpec((1, rows, tile), lambda j, f, s: (f, 0, j)),
            scratch_shapes=[
                pltpu.VMEM((channels, tile), jnp.int32),
                pltpu.VMEM((channels, tile), jnp.bfloat16),
                pltpu.VMEM((channels, tile), jnp.bfloat16),
            ],
        ),
        compiler_params=pltpu.CompilerParams(vmem_limit_bytes=48 * 2**20),
    )(own_bins, coords.T, directions, received)


def steering_kernel(bins_ref, coords_ref, directions_ref, out_ref, offsets_ref):
    sine, cosine = half_angle_fit()
    channels = out_ref.shape[2]
    step = 16

    @pl.when(pl.program_id(1) == 0)
    def _():
        @pl.loop(0, channels, step=step)
        def _(at):
            piece = pl.ds(at, step)
            offsets_ref[piece, :] = (
                coords_ref[piece, 0:1] * directions_ref[0:1, :] + coords_ref[piece, 1:2] * directions_ref[1:2, :]
            )

    turn = bins_ref[pl.program_id(1)] * (2**32 // PHASE_STEPS)
    for at in range(0, channels, step):
        x = (offsets_ref[at : at + step, :] * turn).astype(jnp.float32) * 2.0**-32
        w = x * x
        s = ((sine[2] * w + sine[1]) * w + sine[0]) * x
        c = ((cosine[3] * w + cosine[2]) * w + cosine[1]) * w + cosine[0]
        out_ref[0, 0, at : at + step, :] = (1.0 - s * s).astype(jnp.bfloat16)
        out_ref[0, 1, at : at + step, :] = (s * c).astype(jnp.bfloat16)


def make_steering(some_bins, coords, directions):
    count = some_bins.shape[0]
    channels, beams = coords.shape[1], directions.shape[1]
    tile = min(BEAM_TILE, beams)
    values = count * channels * beams
    return pl.pallas_call(
        steering_kernel,
        out_shape=jax.ShapeDtypeStruct((count, 2, channels, beams), jnp.bfloat16),
        grid_spec=pltpu.PrefetchScalarGridSpec(
            num_scalar_prefetch=1,
            grid=(beams // tile, count),
            in_specs=[
                pl.BlockSpec((channels, 2), lambda j, f, s: (0, 0)),
                pl.BlockSpec((2, tile), lambda j, f, s: (0, j)),
            ],
            out_specs=pl.BlockSpec((1, 2, channels, tile), lambda j, f, s: (f, 0, 0, j)),
            scratch_shapes=[pltpu.VMEM((channels, tile), jnp.int32)],
        ),
        compiler_params=pltpu.CompilerParams(vmem_limit_bytes=32 * 2**20),
        cost_estimate=pl.CostEstimate(flops=20 * values, bytes_accessed=4 * values, transcendentals=2 * values),
    )(some_bins, coords.T, directions)


def product_kernel(at_ref, steering_ref, own_ref, other_ref, own_out_ref, other_out_ref, *, scale):
    sources, _, rows, _ = own_ref.shape
    frames = rows // 2
    left = jnp.concatenate(
        [jnp.concatenate([ref[k, 0] for k in range(sources)], axis=1) for ref in (own_ref, other_ref)], axis=0
    )
    by_cos = jnp.dot(left, steering_ref[0, 0], preferred_element_type=jnp.float32)
    by_sin = jnp.dot(left, steering_ref[0, 1], preferred_element_type=jnp.float32)
    for k, ref in enumerate((own_out_ref, other_out_ref)):
        real, imag = slice(k * rows, k * rows + frames), slice(k * rows + frames, (k + 1) * rows)
        ref[0, :frames, :] = (by_cos[real] - by_sin[imag]) * scale
        ref[0, frames:, :] = (by_cos[imag] + by_sin[real]) * scale


def multiply(first_own, first, count, steering, received, partner):
    sources, _, rows, width = received.shape
    channels, beams = steering.shape[2:]
    tile = min(BEAM_TILE, beams)
    block = (sources, 1, rows, width)
    out = jax.ShapeDtypeStruct((count, rows, beams), jnp.float32)
    out_spec = pl.BlockSpec((1, rows, tile), lambda f, j, s: (f, 0, j))
    return pl.pallas_call(
        functools.partial(product_kernel, scale=1.0 / math.sqrt(channels)),
        out_shape=(out, out),
        grid_spec=pltpu.PrefetchScalarGridSpec(
            num_scalar_prefetch=1,
            grid=(count, beams // tile),
            in_specs=[
                pl.BlockSpec((1, 2, channels, tile), lambda f, j, s: (first + f, 0, 0, j)),
                pl.BlockSpec(block, lambda f, j, s: (0, s[0] + first + f, 0, 0)),
                pl.BlockSpec(block, lambda f, j, s: (0, first + f, 0, 0)),
            ],
            out_specs=(out_spec, out_spec),
        ),
        compiler_params=pltpu.CompilerParams(vmem_limit_bytes=32 * 2**20),
        cost_estimate=pl.CostEstimate(
            flops=8 * count * rows * channels * beams,
            bytes_accessed=count * beams * (4 * channels + 8 * rows),
            transcendentals=0,
        ),
    )(first_own[None], steering, received, partner)


def shared_beams(own_bins, coords, directions, rows):
    tm_count = lax.axis_size("tm")
    core = lax.rem(lax.axis_index("tm"), 2)
    swap = [(i, i ^ 1) for i in range(tm_count)]
    half = own_bins.shape[0] // 2
    received = lax.all_to_all(rows, "chan", 0, 0)
    some_bins = lax.dynamic_slice_in_dim(own_bins, core * half, half, 0)
    steering = make_steering(some_bins, coords, directions)
    partner = lax.ppermute(lax.dynamic_slice_in_dim(received, (1 - core) * half, half, 1), "tm", swap)
    kept, swapped = [], []
    first = 0
    for count in (half - half // 2, half // 2):
        if count == 0:
            continue
        own, other = multiply(core * half, first, count, steering, received, partner)
        kept.append(own)
        swapped.append(lax.ppermute(other, "tm", swap))
        first += count
    return jnp.where(core == 0, jnp.concatenate(kept + swapped), jnp.concatenate(swapped + kept))


def on_device(waveform, coords, directions, bins):
    channels_dev = waveform.shape[0]
    hop_length = FL // 2
    frames_dev = waveform.shape[1] // hop_length
    chan_count = lax.axis_size("chan")
    tm_count = lax.axis_size("tm")
    bins_dev = bins.shape[0] // chan_count
    following = lax.ppermute(
        waveform[:, :hop_length], "tm", [(i, i - 1) for i in range(1, tm_count)]
    )
    table = dft_table(bins, FL)
    rows = spectra_rows(table, waveform, following)
    rows = rows.reshape(chan_count, bins_dev, 2 * frames_dev, channels_dev)
    coords, rows = lax.optimization_barrier((coords, rows))
    own_bins = lax.dynamic_slice_in_dim(bins, lax.axis_index("chan") * bins_dev, bins_dev, 0)
    if bins_dev % 2 == 0 and tm_count % 2 == 0:
        beams = shared_beams(own_bins, coords, directions, rows)
    else:
        received = lax.all_to_all(rows, "chan", 0, 0)
        beams = form_beams(own_bins, coords, directions, received)
    return beams.reshape(bins_dev, 2, frames_dev, directions.shape[1])


def solution(mesh):
    return jax.shard_map(
        on_device,
        mesh=mesh,
        in_specs=(P("chan", "tm"), P(), P(), P()),
        out_specs=P("chan", None, "tm", None),
        check_vma=False,
    )
```

```python
import functools
import math

import jax
import jax.numpy as jnp
import numpy as np
from jax import lax
from jax.experimental import pallas as pl
from jax.experimental.pallas import tpu as pltpu
from jax.sharding import PartitionSpec as P

FL = 1024
PHASE_STEPS = 1048576
LANES = 128
BEAM_TILE = 512


def half_angle_fit():
    r = 0.5 * np.cos(np.pi * (np.arange(2000) + 0.5) / 4000)
    w = r * r
    sine = np.polynomial.polynomial.polyfit(w, np.sqrt(2) * np.sin(np.pi * r) / r, 2)
    cosine = np.polynomial.polynomial.polyfit(w, np.sqrt(2) * np.cos(np.pi * r), 3)
    return [float(c) for c in sine], [float(c) for c in cosine]


def nearest_rest(turns):
    anchor = jnp.float32(1.5 * 2**23)
    return turns - ((turns + anchor) - anchor)


def dft_table(bins, frame_length):
    sample_index = jnp.arange(frame_length, dtype=jnp.int32)
    product = jnp.mod(bins[:, None] * sample_index[None, :], frame_length)
    angle = product.astype(jnp.float32) * jnp.float32(2.0 * math.pi / frame_length)
    window = 0.5 - 0.5 * jnp.cos(
        sample_index.astype(jnp.float32) * jnp.float32(2.0 * math.pi / frame_length)
    )
    scaled = window[None, :]
    norm_factor = jnp.float32(1.0 / math.sqrt(frame_length))
    real_rows = scaled * jnp.cos(angle) * norm_factor
    imag_rows = -scaled * jnp.sin(angle) * norm_factor
    return jnp.concatenate([real_rows, imag_rows], axis=0).astype(jnp.bfloat16)


def spectra_kernel(table_ref, wave_ref, next_ref, out_ref, rows_ref):
    hop = FL // 2
    frames = wave_ref.shape[1] // hop
    bin_count = table_ref.shape[0] // 2
    for t in range(frames):
        if t < frames - 1:
            frame = wave_ref[:, t * hop : t * hop + FL]
        else:
            frame = jnp.concatenate([wave_ref[:, t * hop :], next_ref[...]], axis=1)
        part = lax.dot_general(
            table_ref[...], frame, (((1,), (1,)), ((), ())), preferred_element_type=jnp.float32
        )
        rows_ref[:, t, :] = part[:bin_count]
        rows_ref[:, frames + t, :] = part[bin_count:]
    out_ref[...] = rows_ref[...].astype(jnp.bfloat16)


def spectra_rows(table, waveform, following):
    channels, samples = waveform.shape
    frames = samples // (FL // 2)
    bin_count = table.shape[0] // 2
    return pl.pallas_call(
        spectra_kernel,
        out_shape=jax.ShapeDtypeStruct((bin_count, 2 * frames, channels), jnp.bfloat16),
        scratch_shapes=[pltpu.VMEM((bin_count, 2 * frames, channels), jnp.float32)],
        compiler_params=pltpu.CompilerParams(vmem_limit_bytes=32 * 2**20),
    )(table, waveform, following)


def beam_kernel(bins_ref, offsets_ref, x_ref, out_ref, cos_ref, sin_ref, *, scale):
    sine, cosine = half_angle_fit()
    sources, _, rows, width = x_ref.shape
    channels = sources * width
    step = 16

    turn = bins_ref[pl.program_id(1)] .astype(jnp.float32)
    frames = rows // 2
    by_cos = jnp.zeros((rows, out_ref.shape[2]), jnp.float32)
    by_sin = jnp.zeros((rows, out_ref.shape[2]), jnp.float32)
    group = 2
    for first in range(0, sources, group):
        for at in range(first * width, (first + group) * width, step):
            x = nearest_rest(offsets_ref[at : at + step, :] * turn)
            w = x * x
            s = ((sine[2] * w + sine[1]) * w + sine[0]) * x
            c = ((cosine[3] * w + cosine[2]) * w + cosine[1]) * w + cosine[0]
            cos_ref[at : at + step, :] = (1.0 - s * s).astype(jnp.bfloat16)
            sin_ref[at : at + step, :] = (s * c).astype(jnp.bfloat16)
        left = jnp.concatenate([x_ref[first + k, 0] for k in range(group)], axis=1)
        rows_of = slice(first * width, (first + group) * width)
        by_cos += jnp.dot(left, cos_ref[rows_of, :], preferred_element_type=jnp.float32)
        by_sin += jnp.dot(left, sin_ref[rows_of, :], preferred_element_type=jnp.float32)
    out_ref[0, :frames, :] = (by_cos[:frames] - by_sin[frames:]) * scale
    out_ref[0, frames:, :] = (by_cos[frames:] + by_sin[:frames]) * scale


def form_beams(own_bins, offsets, received):
    sources, bins_dev, rows, width = received.shape
    channels = sources * width
    beams = offsets.shape[1]
    tile = min(BEAM_TILE, beams)
    scale = 1.0 / math.sqrt(channels)
    return pl.pallas_call(
        functools.partial(beam_kernel, scale=scale),
        out_shape=jax.ShapeDtypeStruct((bins_dev, rows, beams), jnp.float32),
        grid_spec=pltpu.PrefetchScalarGridSpec(
            num_scalar_prefetch=1,
            grid=(beams // tile, bins_dev),
            in_specs=[
                pl.BlockSpec((channels, tile), lambda j, f, s: (0, j)),
                pl.BlockSpec((sources, 1, rows, width), lambda j, f, s: (0, f, 0, 0)),
            ],
            out_specs=pl.BlockSpec((1, rows, tile), lambda j, f, s: (f, 0, j)),
            scratch_shapes=[
                pltpu.VMEM((channels, tile), jnp.bfloat16),
                pltpu.VMEM((channels, tile), jnp.bfloat16),
            ],
        ),
        compiler_params=pltpu.CompilerParams(vmem_limit_bytes=48 * 2**20),
    )(own_bins, offsets, received)


def steering_kernel(bins_ref, offsets_ref, out_ref):
    sine, cosine = half_angle_fit()
    channels = out_ref.shape[3]
    step = 16

    turn = bins_ref[pl.program_id(1)] .astype(jnp.float32)
    for at in range(0, channels, step):
        x = nearest_rest(offsets_ref[at : at + step, :] * turn)
        w = x * x
        s = ((sine[2] * w + sine[1]) * w + sine[0]) * x
        c = ((cosine[3] * w + cosine[2]) * w + cosine[1]) * w + cosine[0]
        out_ref[0, 0, 0, at : at + step, :] = (1.0 - s * s).astype(jnp.bfloat16)
        out_ref[0, 0, 1, at : at + step, :] = (s * c).astype(jnp.bfloat16)


def make_steering(some_bins, offsets):
    count = some_bins.shape[0]
    channels, beams = offsets.shape
    tile = min(BEAM_TILE, beams)
    values = count * channels * beams
    return pl.pallas_call(
        steering_kernel,
        out_shape=jax.ShapeDtypeStruct((count, beams // tile, 2, channels, tile), jnp.bfloat16),
        grid_spec=pltpu.PrefetchScalarGridSpec(
            num_scalar_prefetch=1,
            grid=(beams // tile, count),
            in_specs=[
                pl.BlockSpec((channels, tile), lambda j, f, s: (0, j)),
            ],
            out_specs=pl.BlockSpec((1, 1, 2, channels, tile), lambda j, f, s: (f, j, 0, 0, 0)),
        ),
        compiler_params=pltpu.CompilerParams(vmem_limit_bytes=32 * 2**20),
        cost_estimate=pl.CostEstimate(flops=20 * values, bytes_accessed=4 * values, transcendentals=2 * values),
    )(some_bins, offsets)


def product_kernel(at_ref, steering_ref, own_ref, other_ref, own_out_ref, other_out_ref, *, scale):
    sources, _, rows, _ = own_ref.shape
    frames = rows // 2
    left = jnp.concatenate(
        [jnp.concatenate([ref[k, 0] for k in range(sources)], axis=1) for ref in (own_ref, other_ref)], axis=0
    )
    by_cos = jnp.dot(left, steering_ref[0, 0, 0], preferred_element_type=jnp.float32)
    by_sin = jnp.dot(left, steering_ref[0, 0, 1], preferred_element_type=jnp.float32)
    for k, ref in enumerate((own_out_ref, other_out_ref)):
        real, imag = slice(k * rows, k * rows + frames), slice(k * rows + frames, (k + 1) * rows)
        ref[0, :frames, :] = (by_cos[real] - by_sin[imag]) * scale
        ref[0, frames:, :] = (by_cos[imag] + by_sin[real]) * scale


def multiply(first_own, first, count, steering, received, partner):
    sources, _, rows, width = received.shape
    _, tiles, _, channels, tile = steering.shape
    beams = tiles * tile
    block = (sources, 1, rows, width)
    out = jax.ShapeDtypeStruct((count, rows, beams), jnp.float32)
    out_spec = pl.BlockSpec((1, rows, tile), lambda f, j, s: (f, 0, j))
    return pl.pallas_call(
        functools.partial(product_kernel, scale=1.0 / math.sqrt(channels)),
        out_shape=(out, out),
        grid_spec=pltpu.PrefetchScalarGridSpec(
            num_scalar_prefetch=1,
            grid=(count, beams // tile),
            in_specs=[
                pl.BlockSpec((1, 1, 2, channels, tile), lambda f, j, s: (first + f, j, 0, 0, 0)),
                pl.BlockSpec(block, lambda f, j, s: (0, s[0] + first + f, 0, 0)),
                pl.BlockSpec(block, lambda f, j, s: (0, first + f, 0, 0)),
            ],
            out_specs=(out_spec, out_spec),
        ),
        compiler_params=pltpu.CompilerParams(vmem_limit_bytes=32 * 2**20),
        cost_estimate=pl.CostEstimate(
            flops=8 * count * rows * channels * beams,
            bytes_accessed=count * beams * (4 * channels + 8 * rows),
            transcendentals=0,
        ),
    )(first_own[None], steering, received, partner)


def give_kernel(at_ref, received_ref, steering_ref, out_ref):
    out_ref[...] = received_ref[...]


def cut_for_other(first_bin, count, received, steering):
    sources, _, rows, width = received.shape
    block = (sources, 1, rows, width)
    return pl.pallas_call(
        give_kernel,
        out_shape=jax.ShapeDtypeStruct((sources, count, rows, width), received.dtype),
        grid_spec=pltpu.PrefetchScalarGridSpec(
            num_scalar_prefetch=1,
            grid=(count,),
            in_specs=[
                pl.BlockSpec(block, lambda f, s: (0, s[0] + f, 0, 0)),
                pl.BlockSpec(memory_space=pl.ANY),
            ],
            out_specs=pl.BlockSpec(block, lambda f, s: (0, f, 0, 0)),
        ),
    )(first_bin[None], received, steering)


def shared_beams(own_bins, offsets, rows):
    tm_count = lax.axis_size("tm")
    core = lax.rem(lax.axis_index("tm"), 2)
    swap = [(i, i ^ 1) for i in range(tm_count)]
    half = own_bins.shape[0] // 2
    received = lax.all_to_all(rows, "chan", 0, 0)
    some_bins = lax.dynamic_slice_in_dim(own_bins, core * half, half, 0)
    steering = make_steering(some_bins, offsets)
    partner = lax.ppermute(cut_for_other((1 - core) * half, half, received, steering), "tm", swap)
    kept, swapped = [], []
    first = 0
    for count in (half - half // 2, half // 2):
        if count == 0:
            continue
        own, other = multiply(core * half, first, count, steering, received, partner)
        kept.append(own)
        swapped.append(lax.ppermute(other, "tm", swap))
        first += count
    return jnp.where(core == 0, jnp.concatenate(kept + swapped), jnp.concatenate(swapped + kept))


def on_device(waveform, coords, directions, bins):
    channels_dev = waveform.shape[0]
    hop_length = FL // 2
    frames_dev = waveform.shape[1] // hop_length
    chan_count = lax.axis_size("chan")
    tm_count = lax.axis_size("tm")
    bins_dev = bins.shape[0] // chan_count
    following = lax.ppermute(
        waveform[:, :hop_length], "tm", [(i, i - 1) for i in range(1, tm_count)]
    )
    table = dft_table(bins, FL)
    rows = spectra_rows(table, waveform, following)
    rows = rows.reshape(chan_count, bins_dev, 2 * frames_dev, channels_dev)
    coords, rows = lax.optimization_barrier((coords, rows))
    offsets = (
        coords[0][:, None] * directions[0][None, :] + coords[1][:, None] * directions[1][None, :]
    ).astype(jnp.float32) * (1.0 / PHASE_STEPS)
    own_bins = lax.dynamic_slice_in_dim(bins, lax.axis_index("chan") * bins_dev, bins_dev, 0)
    if bins_dev % 2 == 0 and tm_count % 2 == 0:
        beams = shared_beams(own_bins, offsets, rows)
    else:
        received = lax.all_to_all(rows, "chan", 0, 0)
        beams = form_beams(own_bins, offsets, received)
    return beams.reshape(bins_dev, 2, frames_dev, directions.shape[1])


def solution(mesh):
    return jax.shard_map(
        on_device,
        mesh=mesh,
        in_specs=(P("chan", "tm"), P(), P(), P()),
        out_specs=P("chan", None, "tm", None),
        check_vma=False,
    )
```

```python
import functools
import math

import jax
import jax.numpy as jnp
import numpy as np
from jax import lax
from jax.experimental import pallas as pl
from jax.experimental.pallas import tpu as pltpu
from jax.sharding import PartitionSpec as P

FL = 1024
PHASE_STEPS = 1048576
LANES = 128
BEAM_TILE = 512


def half_angle_fit():
    r = 0.5 * np.cos(np.pi * (np.arange(2000) + 0.5) / 4000)
    w = r * r
    sine = np.polynomial.polynomial.polyfit(w, np.sqrt(2) * np.sin(np.pi * r) / r, 2)
    cosine = np.polynomial.polynomial.polyfit(w, np.sqrt(2) * np.cos(np.pi * r), 3)
    return [float(c) for c in sine], [float(c) for c in cosine]


def nearest_rest(turns):
    anchor = jnp.float32(1.5 * 2**23)
    return turns - ((turns + anchor) - anchor)


def dft_table(bins, frame_length):
    sample_index = jnp.arange(frame_length, dtype=jnp.int32)
    product = jnp.mod(bins[:, None] * sample_index[None, :], frame_length)
    angle = product.astype(jnp.float32) * jnp.float32(2.0 * math.pi / frame_length)
    window = 0.5 - 0.5 * jnp.cos(
        sample_index.astype(jnp.float32) * jnp.float32(2.0 * math.pi / frame_length)
    )
    scaled = window[None, :]
    norm_factor = jnp.float32(1.0 / math.sqrt(frame_length))
    real_rows = scaled * jnp.cos(angle) * norm_factor
    imag_rows = -scaled * jnp.sin(angle) * norm_factor
    return jnp.concatenate([real_rows, imag_rows], axis=0).astype(jnp.bfloat16)


def spectra_kernel(table_ref, wave_ref, next_ref, out_ref, rows_ref):
    hop = FL // 2
    frames = wave_ref.shape[1] // hop
    bin_count = table_ref.shape[0] // 2
    for t in range(frames):
        if t < frames - 1:
            frame = wave_ref[:, t * hop : t * hop + FL]
        else:
            frame = jnp.concatenate([wave_ref[:, t * hop :], next_ref[...]], axis=1)
        part = lax.dot_general(
            table_ref[...], frame, (((1,), (1,)), ((), ())), preferred_element_type=jnp.float32
        )
        rows_ref[:, t, :] = part[:bin_count]
        rows_ref[:, frames + t, :] = part[bin_count:]
    out_ref[...] = rows_ref[...].astype(jnp.bfloat16)


def spectra_rows(table, waveform, following):
    channels, samples = waveform.shape
    frames = samples // (FL // 2)
    bin_count = table.shape[0] // 2
    return pl.pallas_call(
        spectra_kernel,
        out_shape=jax.ShapeDtypeStruct((bin_count, 2 * frames, channels), jnp.bfloat16),
        scratch_shapes=[pltpu.VMEM((bin_count, 2 * frames, channels), jnp.float32)],
        compiler_params=pltpu.CompilerParams(vmem_limit_bytes=32 * 2**20),
    )(table, waveform, following)


def beam_kernel(bins_ref, offsets_ref, x_ref, out_ref, cos_ref, sin_ref, *, scale):
    sine, cosine = half_angle_fit()
    sources, _, rows, width = x_ref.shape
    channels = sources * width
    step = 16

    turn = bins_ref[pl.program_id(1)] .astype(jnp.float32)
    frames = rows // 2
    by_cos = jnp.zeros((rows, out_ref.shape[2]), jnp.float32)
    by_sin = jnp.zeros((rows, out_ref.shape[2]), jnp.float32)
    group = 2
    for first in range(0, sources, group):
        for at in range(first * width, (first + group) * width, step):
            x = nearest_rest(offsets_ref[at : at + step, :] * turn)
            w = x * x
            s = ((sine[2] * w + sine[1]) * w + sine[0]) * x
            c = ((cosine[3] * w + cosine[2]) * w + cosine[1]) * w + cosine[0]
            cos_ref[at : at + step, :] = (1.0 - s * s).astype(jnp.bfloat16)
            sin_ref[at : at + step, :] = (s * c).astype(jnp.bfloat16)
        left = jnp.concatenate([x_ref[first + k, 0] for k in range(group)], axis=1)
        rows_of = slice(first * width, (first + group) * width)
        by_cos += jnp.dot(left, cos_ref[rows_of, :], preferred_element_type=jnp.float32)
        by_sin += jnp.dot(left, sin_ref[rows_of, :], preferred_element_type=jnp.float32)
    out_ref[0, :frames, :] = (by_cos[:frames] - by_sin[frames:]) * scale
    out_ref[0, frames:, :] = (by_cos[frames:] + by_sin[:frames]) * scale


def form_beams(own_bins, offsets, received):
    sources, bins_dev, rows, width = received.shape
    channels = sources * width
    beams = offsets.shape[1]
    tile = min(BEAM_TILE, beams)
    scale = 1.0 / math.sqrt(channels)
    return pl.pallas_call(
        functools.partial(beam_kernel, scale=scale),
        out_shape=jax.ShapeDtypeStruct((bins_dev, rows, beams), jnp.float32),
        grid_spec=pltpu.PrefetchScalarGridSpec(
            num_scalar_prefetch=1,
            grid=(beams // tile, bins_dev),
            in_specs=[
                pl.BlockSpec((channels, tile), lambda j, f, s: (0, j)),
                pl.BlockSpec((sources, 1, rows, width), lambda j, f, s: (0, f, 0, 0)),
            ],
            out_specs=pl.BlockSpec((1, rows, tile), lambda j, f, s: (f, 0, j)),
            scratch_shapes=[
                pltpu.VMEM((channels, tile), jnp.bfloat16),
                pltpu.VMEM((channels, tile), jnp.bfloat16),
            ],
        ),
        compiler_params=pltpu.CompilerParams(vmem_limit_bytes=48 * 2**20),
    )(own_bins, offsets, received)


def steering_kernel(bins_ref, offsets_ref, out_ref):
    sine, cosine = half_angle_fit()
    channels = out_ref.shape[3]
    step = 16

    turn = bins_ref[pl.program_id(1)] .astype(jnp.float32)
    for at in range(0, channels, step):
        x = nearest_rest(offsets_ref[at : at + step, :] * turn)
        w = x * x
        s = ((sine[2] * w + sine[1]) * w + sine[0]) * x
        c = ((cosine[3] * w + cosine[2]) * w + cosine[1]) * w + cosine[0]
        out_ref[0, 0, 0, at : at + step, :] = (1.0 - s * s).astype(jnp.bfloat16)
        out_ref[0, 0, 1, at : at + step, :] = (s * c).astype(jnp.bfloat16)


def make_steering(some_bins, offsets):
    count = some_bins.shape[0]
    channels, beams = offsets.shape
    tile = min(BEAM_TILE, beams)
    values = count * channels * beams
    return pl.pallas_call(
        steering_kernel,
        out_shape=jax.ShapeDtypeStruct((count, beams // tile, 2, channels, tile), jnp.bfloat16),
        grid_spec=pltpu.PrefetchScalarGridSpec(
            num_scalar_prefetch=1,
            grid=(beams // tile, count),
            in_specs=[
                pl.BlockSpec((channels, tile), lambda j, f, s: (0, j)),
            ],
            out_specs=pl.BlockSpec((1, 1, 2, channels, tile), lambda j, f, s: (f, j, 0, 0, 0)),
        ),
        compiler_params=pltpu.CompilerParams(vmem_limit_bytes=32 * 2**20),
        cost_estimate=pl.CostEstimate(flops=20 * values, bytes_accessed=4 * values, transcendentals=2 * values),
    )(some_bins, offsets)


def product_kernel(at_ref, steering_ref, own_ref, other_ref, own_out_ref, other_out_ref, *, scale):
    sources, _, rows, _ = own_ref.shape
    frames = rows // 2
    left = jnp.concatenate(
        [jnp.concatenate([ref[k, 0] for k in range(sources)], axis=1) for ref in (own_ref, other_ref)], axis=0
    )
    by_cos = jnp.dot(left, steering_ref[0, 0, 0], preferred_element_type=jnp.float32)
    by_sin = jnp.dot(left, steering_ref[0, 0, 1], preferred_element_type=jnp.float32)
    for k, ref in enumerate((own_out_ref, other_out_ref)):
        real, imag = slice(k * rows, k * rows + frames), slice(k * rows + frames, (k + 1) * rows)
        ref[0, :frames, :] = (by_cos[real] - by_sin[imag]) * scale
        ref[0, frames:, :] = (by_cos[imag] + by_sin[real]) * scale


def multiply(first_own, first, count, steering, received, partner):
    sources, _, rows, width = received.shape
    _, tiles, _, channels, tile = steering.shape
    beams = tiles * tile
    block = (sources, 1, rows, width)
    out = jax.ShapeDtypeStruct((count, rows, beams), jnp.float32)
    out_spec = pl.BlockSpec((1, rows, tile), lambda f, j, s: (f, 0, j))
    return pl.pallas_call(
        functools.partial(product_kernel, scale=1.0 / math.sqrt(channels)),
        out_shape=(out, out),
        grid_spec=pltpu.PrefetchScalarGridSpec(
            num_scalar_prefetch=1,
            grid=(count, beams // tile),
            in_specs=[
                pl.BlockSpec((1, 1, 2, channels, tile), lambda f, j, s: (first + f, j, 0, 0, 0)),
                pl.BlockSpec(block, lambda f, j, s: (0, s[0] + first + f, 0, 0)),
                pl.BlockSpec(block, lambda f, j, s: (0, first + f, 0, 0)),
            ],
            out_specs=(out_spec, out_spec),
        ),
        compiler_params=pltpu.CompilerParams(vmem_limit_bytes=32 * 2**20),
        cost_estimate=pl.CostEstimate(
            flops=8 * count * rows * channels * beams,
            bytes_accessed=count * beams * (4 * channels + 8 * rows),
            transcendentals=0,
        ),
    )(first_own[None], steering, received, partner)


def give_kernel(at_ref, received_ref, steering_ref, out_ref):
    out_ref[...] = received_ref[...]


def cut_for_other(half_index, count, received, steering):
    sources, _, rows, width = received.shape
    block = (sources, count, rows, width)
    return pl.pallas_call(
        give_kernel,
        out_shape=jax.ShapeDtypeStruct((sources, count, rows, width), received.dtype),
        grid_spec=pltpu.PrefetchScalarGridSpec(
            num_scalar_prefetch=1,
            grid=(1,),
            in_specs=[
                pl.BlockSpec(block, lambda f, s: (0, s[0], 0, 0)),
                pl.BlockSpec(memory_space=pl.ANY),
            ],
            out_specs=pl.BlockSpec(block, lambda f, s: (0, 0, 0, 0)),
        ),
    )(half_index[None], received, steering)


def shared_beams(own_bins, offsets, rows):
    tm_count = lax.axis_size("tm")
    core = lax.rem(lax.axis_index("tm"), 2)
    swap = [(i, i ^ 1) for i in range(tm_count)]
    half = own_bins.shape[0] // 2
    received = lax.all_to_all(rows, "chan", 0, 0)
    some_bins = lax.dynamic_slice_in_dim(own_bins, core * half, half, 0)
    steering = make_steering(some_bins, offsets)
    partner = lax.ppermute(cut_for_other(1 - core, half, received, steering), "tm", swap)
    kept, swapped = [], []
    first = 0
    for count in (half - half // 2, half // 2):
        if count == 0:
            continue
        own, other = multiply(core * half, first, count, steering, received, partner)
        kept.append(own)
        swapped.append(lax.ppermute(other, "tm", swap))
        first += count
    return jnp.where(core == 0, jnp.concatenate(kept + swapped), jnp.concatenate(swapped + kept))


def on_device(waveform, coords, directions, bins):
    channels_dev = waveform.shape[0]
    hop_length = FL // 2
    frames_dev = waveform.shape[1] // hop_length
    chan_count = lax.axis_size("chan")
    tm_count = lax.axis_size("tm")
    bins_dev = bins.shape[0] // chan_count
    following = lax.ppermute(
        waveform[:, :hop_length], "tm", [(i, i - 1) for i in range(1, tm_count)]
    )
    table = dft_table(bins, FL)
    rows = spectra_rows(table, waveform, following)
    rows = rows.reshape(chan_count, bins_dev, 2 * frames_dev, channels_dev)
    coords, rows = lax.optimization_barrier((coords, rows))
    offsets = (
        coords[0][:, None] * directions[0][None, :] + coords[1][:, None] * directions[1][None, :]
    ).astype(jnp.float32) * (1.0 / PHASE_STEPS)
    own_bins = lax.dynamic_slice_in_dim(bins, lax.axis_index("chan") * bins_dev, bins_dev, 0)
    if bins_dev % 2 == 0 and tm_count % 2 == 0:
        beams = shared_beams(own_bins, offsets, rows)
    else:
        received = lax.all_to_all(rows, "chan", 0, 0)
        beams = form_beams(own_bins, offsets, received)
    return beams.reshape(bins_dev, 2, frames_dev, directions.shape[1])


def solution(mesh):
    return jax.shard_map(
        on_device,
        mesh=mesh,
        in_specs=(P("chan", "tm"), P(), P(), P()),
        out_specs=P("chan", None, "tm", None),
        check_vma=False,
    )
```

```python
import functools
import math

import jax
import jax.numpy as jnp
import numpy as np
from jax import lax
from jax.experimental import pallas as pl
from jax.experimental.pallas import tpu as pltpu
from jax.sharding import PartitionSpec as P

FL = 1024
PHASE_STEPS = 1048576
LANES = 128
BEAM_TILE = 512


def half_angle_fit():
    r = 0.5 * np.cos(np.pi * (np.arange(2000) + 0.5) / 4000)
    w = r * r
    sine = np.polynomial.polynomial.polyfit(w, np.sqrt(2) * np.sin(np.pi * r) / r, 2)
    cosine = np.polynomial.polynomial.polyfit(w, np.sqrt(2) * np.cos(np.pi * r), 3)
    return [float(c) for c in sine], [float(c) for c in cosine]


def nearest_rest(turns):
    anchor = jnp.float32(1.5 * 2**23)
    return turns - ((turns + anchor) - anchor)


def dft_table(bins, frame_length):
    sample_index = jnp.arange(frame_length, dtype=jnp.int32)
    product = jnp.mod(bins[:, None] * sample_index[None, :], frame_length)
    angle = product.astype(jnp.float32) * jnp.float32(2.0 * math.pi / frame_length)
    window = 0.5 - 0.5 * jnp.cos(
        sample_index.astype(jnp.float32) * jnp.float32(2.0 * math.pi / frame_length)
    )
    scaled = window[None, :]
    norm_factor = jnp.float32(1.0 / math.sqrt(frame_length))
    real_rows = scaled * jnp.cos(angle) * norm_factor
    imag_rows = -scaled * jnp.sin(angle) * norm_factor
    return jnp.concatenate([real_rows, imag_rows], axis=0).astype(jnp.bfloat16)


def spectra_kernel(table_ref, wave_ref, next_ref, out_ref, rows_ref):
    hop = FL // 2
    frames = wave_ref.shape[1] // hop
    bin_count = table_ref.shape[0] // 2
    for t in range(frames):
        if t < frames - 1:
            frame = wave_ref[:, t * hop : t * hop + FL]
        else:
            frame = jnp.concatenate([wave_ref[:, t * hop :], next_ref[...]], axis=1)
        part = lax.dot_general(
            table_ref[...], frame, (((1,), (1,)), ((), ())), preferred_element_type=jnp.float32
        )
        rows_ref[:, t, :] = part[:bin_count]
        rows_ref[:, frames + t, :] = part[bin_count:]
    out_ref[...] = rows_ref[...].astype(jnp.bfloat16)


def spectra_rows(table, waveform, following):
    channels, samples = waveform.shape
    frames = samples // (FL // 2)
    bin_count = table.shape[0] // 2
    return pl.pallas_call(
        spectra_kernel,
        out_shape=jax.ShapeDtypeStruct((bin_count, 2 * frames, channels), jnp.bfloat16),
        scratch_shapes=[pltpu.VMEM((bin_count, 2 * frames, channels), jnp.float32)],
        compiler_params=pltpu.CompilerParams(vmem_limit_bytes=32 * 2**20),
    )(table, waveform, following)


def beam_kernel(bins_ref, offsets_ref, x_ref, out_ref, cos_ref, sin_ref, *, scale):
    sine, cosine = half_angle_fit()
    sources, _, rows, width = x_ref.shape
    channels = sources * width
    step = 16

    turn = bins_ref[pl.program_id(1)] .astype(jnp.float32)
    frames = rows // 2
    by_cos = jnp.zeros((rows, out_ref.shape[2]), jnp.float32)
    by_sin = jnp.zeros((rows, out_ref.shape[2]), jnp.float32)
    group = 2
    for first in range(0, sources, group):
        for at in range(first * width, (first + group) * width, step):
            x = nearest_rest(offsets_ref[at : at + step, :] * turn)
            w = x * x
            s = ((sine[2] * w + sine[1]) * w + sine[0]) * x
            c = ((cosine[3] * w + cosine[2]) * w + cosine[1]) * w + cosine[0]
            cos_ref[at : at + step, :] = (1.0 - s * s).astype(jnp.bfloat16)
            sin_ref[at : at + step, :] = (s * c).astype(jnp.bfloat16)
        left = jnp.concatenate([x_ref[first + k, 0] for k in range(group)], axis=1)
        rows_of = slice(first * width, (first + group) * width)
        by_cos += jnp.dot(left, cos_ref[rows_of, :], preferred_element_type=jnp.float32)
        by_sin += jnp.dot(left, sin_ref[rows_of, :], preferred_element_type=jnp.float32)
    out_ref[0, :frames, :] = (by_cos[:frames] - by_sin[frames:]) * scale
    out_ref[0, frames:, :] = (by_cos[frames:] + by_sin[:frames]) * scale


def form_beams(own_bins, offsets, received):
    sources, bins_dev, rows, width = received.shape
    channels = sources * width
    beams = offsets.shape[1]
    tile = min(BEAM_TILE, beams)
    scale = 1.0 / math.sqrt(channels)
    return pl.pallas_call(
        functools.partial(beam_kernel, scale=scale),
        out_shape=jax.ShapeDtypeStruct((bins_dev, rows, beams), jnp.float32),
        grid_spec=pltpu.PrefetchScalarGridSpec(
            num_scalar_prefetch=1,
            grid=(beams // tile, bins_dev),
            in_specs=[
                pl.BlockSpec((channels, tile), lambda j, f, s: (0, j)),
                pl.BlockSpec((sources, 1, rows, width), lambda j, f, s: (0, f, 0, 0)),
            ],
            out_specs=pl.BlockSpec((1, rows, tile), lambda j, f, s: (f, 0, j)),
            scratch_shapes=[
                pltpu.VMEM((channels, tile), jnp.bfloat16),
                pltpu.VMEM((channels, tile), jnp.bfloat16),
            ],
        ),
        compiler_params=pltpu.CompilerParams(vmem_limit_bytes=48 * 2**20),
    )(own_bins, offsets, received)


def steering_kernel(bins_ref, offsets_ref, out_ref):
    sine, cosine = half_angle_fit()
    channels = out_ref.shape[3]
    step = 16

    turn = bins_ref[pl.program_id(1)] .astype(jnp.float32)
    for at in range(0, channels, step):
        x = nearest_rest(offsets_ref[at : at + step, :] * turn)
        w = x * x
        s = ((sine[2] * w + sine[1]) * w + sine[0]) * x
        c = ((cosine[3] * w + cosine[2]) * w + cosine[1]) * w + cosine[0]
        out_ref[0, 0, 0, at : at + step, :] = (1.0 - s * s).astype(jnp.bfloat16)
        out_ref[0, 0, 1, at : at + step, :] = (s * c).astype(jnp.bfloat16)


def make_steering(some_bins, offsets):
    count = some_bins.shape[0]
    channels, beams = offsets.shape
    tile = min(BEAM_TILE, beams)
    values = count * channels * beams
    return pl.pallas_call(
        steering_kernel,
        out_shape=jax.ShapeDtypeStruct((count, beams // tile, 2, channels, tile), jnp.bfloat16),
        grid_spec=pltpu.PrefetchScalarGridSpec(
            num_scalar_prefetch=1,
            grid=(beams // tile, count),
            in_specs=[
                pl.BlockSpec((channels, tile), lambda j, f, s: (0, j)),
            ],
            out_specs=pl.BlockSpec((1, 1, 2, channels, tile), lambda j, f, s: (f, j, 0, 0, 0)),
        ),
        compiler_params=pltpu.CompilerParams(vmem_limit_bytes=32 * 2**20),
        cost_estimate=pl.CostEstimate(flops=20 * values, bytes_accessed=4 * values, transcendentals=2 * values),
    )(some_bins, offsets)


def product_kernel(at_ref, steering_ref, own_ref, other_ref, own_out_ref, other_out_ref, *, scale):
    sources, _, rows, _ = own_ref.shape
    frames = rows // 2
    left = jnp.concatenate(
        [jnp.concatenate([ref[k, 0] for k in range(sources)], axis=1) for ref in (own_ref, other_ref)], axis=0
    )
    by_cos = jnp.dot(left, steering_ref[0, 0, 0], preferred_element_type=jnp.float32)
    by_sin = jnp.dot(left, steering_ref[0, 0, 1], preferred_element_type=jnp.float32)
    for k, ref in enumerate((own_out_ref, other_out_ref)):
        real, imag = slice(k * rows, k * rows + frames), slice(k * rows + frames, (k + 1) * rows)
        ref[0, :frames, :] = (by_cos[real] - by_sin[imag]) * scale
        ref[0, frames:, :] = (by_cos[imag] + by_sin[real]) * scale


def multiply(first_own, first, count, steering, received, partner):
    sources, _, rows, width = received.shape
    _, tiles, _, channels, tile = steering.shape
    beams = tiles * tile
    block = (sources, 1, rows, width)
    out = jax.ShapeDtypeStruct((count, rows, beams), jnp.float32)
    out_spec = pl.BlockSpec((1, rows, tile), lambda f, j, s: (f, 0, j))
    return pl.pallas_call(
        functools.partial(product_kernel, scale=1.0 / math.sqrt(channels)),
        out_shape=(out, out),
        grid_spec=pltpu.PrefetchScalarGridSpec(
            num_scalar_prefetch=1,
            grid=(count, beams // tile),
            in_specs=[
                pl.BlockSpec((1, 1, 2, channels, tile), lambda f, j, s: (f, j, 0, 0, 0)),
                pl.BlockSpec(block, lambda f, j, s: (0, s[0] + first + f, 0, 0)),
                pl.BlockSpec(block, lambda f, j, s: (0, first + f, 0, 0)),
            ],
            out_specs=(out_spec, out_spec),
        ),
        compiler_params=pltpu.CompilerParams(vmem_limit_bytes=32 * 2**20),
        cost_estimate=pl.CostEstimate(
            flops=8 * count * rows * channels * beams,
            bytes_accessed=count * beams * (4 * channels + 8 * rows),
            transcendentals=0,
        ),
    )(first_own[None], steering, received, partner)


def give_kernel(at_ref, received_ref, steering_ref, out_ref):
    out_ref[...] = received_ref[...]


def cut_for_other(half_index, count, received, steering):
    sources, _, rows, width = received.shape
    block = (sources, count, rows, width)
    return pl.pallas_call(
        give_kernel,
        out_shape=jax.ShapeDtypeStruct((sources, count, rows, width), received.dtype),
        grid_spec=pltpu.PrefetchScalarGridSpec(
            num_scalar_prefetch=1,
            grid=(1,),
            in_specs=[
                pl.BlockSpec(block, lambda f, s: (0, s[0], 0, 0)),
                pl.BlockSpec(memory_space=pl.ANY),
            ],
            out_specs=pl.BlockSpec(block, lambda f, s: (0, 0, 0, 0)),
        ),
    )(half_index[None], received, steering)


def shared_beams(own_bins, offsets, rows):
    tm_count = lax.axis_size("tm")
    core = lax.rem(lax.axis_index("tm"), 2)
    swap = [(i, i ^ 1) for i in range(tm_count)]
    half = own_bins.shape[0] // 2
    received = lax.all_to_all(rows, "chan", 0, 0)
    some_bins = lax.dynamic_slice_in_dim(own_bins, core * half, half, 0)
    counts = [count for count in (half - 1, 1) if count]
    steering = [
        make_steering(some_bins[k * counts[0] : k * counts[0] + count], offsets) for k, count in enumerate(counts)
    ]
    partner = lax.ppermute(cut_for_other(1 - core, half, received, steering[0]), "tm", swap)
    kept, swapped = [], []
    first = 0
    for count, part in zip(counts, steering):
        own, other = multiply(core * half, first, count, part, received, partner)
        kept.append(own)
        swapped.append(lax.ppermute(other, "tm", swap))
        first += count
    return jnp.where(core == 0, jnp.concatenate(kept + swapped), jnp.concatenate(swapped + kept))


def on_device(waveform, coords, directions, bins):
    channels_dev = waveform.shape[0]
    hop_length = FL // 2
    frames_dev = waveform.shape[1] // hop_length
    chan_count = lax.axis_size("chan")
    tm_count = lax.axis_size("tm")
    bins_dev = bins.shape[0] // chan_count
    following = lax.ppermute(
        waveform[:, :hop_length], "tm", [(i, i - 1) for i in range(1, tm_count)]
    )
    table = dft_table(bins, FL)
    rows = spectra_rows(table, waveform, following)
    rows = rows.reshape(chan_count, bins_dev, 2 * frames_dev, channels_dev)
    coords, rows = lax.optimization_barrier((coords, rows))
    offsets = (
        coords[0][:, None] * directions[0][None, :] + coords[1][:, None] * directions[1][None, :]
    ).astype(jnp.float32) * (1.0 / PHASE_STEPS)
    own_bins = lax.dynamic_slice_in_dim(bins, lax.axis_index("chan") * bins_dev, bins_dev, 0)
    if bins_dev % 2 == 0 and tm_count % 2 == 0:
        beams = shared_beams(own_bins, offsets, rows)
    else:
        received = lax.all_to_all(rows, "chan", 0, 0)
        beams = form_beams(own_bins, offsets, received)
    return beams.reshape(bins_dev, 2, frames_dev, directions.shape[1])


def solution(mesh):
    return jax.shard_map(
        on_device,
        mesh=mesh,
        in_specs=(P("chan", "tm"), P(), P(), P()),
        out_specs=P("chan", None, "tm", None),
        check_vma=False,
    )
```
